512 devices in a mesh: dp: 128 (over y, z, core), seq: 4 (over x).
Axes of the slice: x: 4, y: 8, z: 8, core: 2. Of those that a mesh axis runs over, the one named last changes fastest.
Arguments:
- residual: bfloat16 [131072, 2048], P(('dp', 'seq')), may hold values from -6 to 6
- queries: bfloat16 [32768, 2048], P(('dp', 'seq'))
- key_proj: bfloat16 [32768, 2048], P(('dp', 'seq'))
- value_proj: bfloat16 [32768, 2048], P(('dp', 'seq')), may hold values from -6 to 6
- out_grad: bfloat16 [32768, 2048], P(('dp', 'seq')), may hold values from -6 to 6
- router: float32 [2048], replicated, may hold values from -0.125 to 0.125
- counts: int32 [128, 4], replicated, may hold values from 1 to 63, as said below
- kept_rows: int32 [128, 4, 64], replicated, may hold values from 0 to 255, as said below
Outputs:
- block_out: bfloat16 [131072, 2048], P(('dp', 'seq'))
- query_grad: bfloat16 [32768, 2048], P(('dp', 'seq'))
- key_grad: bfloat16 [32768, 2048], P(('dp', 'seq'))
- value_grad: bfloat16 [32768, 2048], P(('dp', 'seq'))
- router_grad: float32 [2048], replicated
The draws below stay inside these ranges and needn't reach their ends.
Inputs may be any that keep to these rules, and one draw needn't show every extreme that they name: Device block (n, b) and block (n + 128 / 2 mod 128, b) have counts that add up to 64. `kept_rows`: for each sequence and block the first counts[n, b] entries are distinct and rising; the other entries are 0.
All inputs are finite; a program needn't handle non-finite values.
Results may differ from the reference program's by a relative error of at most 0.0058.
Values may be sent and summed in bfloat16 or wider, within the bound.
No kernel may reach another device: no remote copies, remote signals or barrier semaphores. Data moves between devices by JAX's collectives and lax.ppermute only.
A program may use at most 64 MiB of HBM per device.

```python
import math
import jax
import jax.numpy as jnp
from jax import lax

HEADS = 16
WIDTH = 2048
TOK_DEV = 256
MEAN_KEPT = 32
CAPACITY = 64
SEQ_LEN = 1024
TOKENS = 131072
KEPT_SLOTS = 32768
N_DP = 128
N_SEQ = 4


def shared_rows(key):
    base = jax.random.normal(jax.random.fold_in(key, 500), (KEPT_SLOTS, WIDTH), jnp.float32)
    return base


def mixed_rows(key, salt):
    base = shared_rows(key)
    key = jax.random.fold_in(key, salt)
    own = jax.random.normal(key, (KEPT_SLOTS, WIDTH), jnp.float32)
    blend = 0.6 * base + 0.8 * own
    return jnp.clip(blend, -16.0, 16.0).astype(jnp.bfloat16)


def draw_queries(key, part):
    return mixed_rows(key, 11)


def draw_key_proj(key, part):
    return mixed_rows(key, 12)


def routing(key):
    half_dp = N_DP // 2
    shift = jax.random.randint(jax.random.fold_in(key, 700), (half_dp, N_SEQ), -(MEAN_KEPT - 1), MEAN_KEPT)
    shift = shift.at[0, 0].set(MEAN_KEPT - 1)
    sign = 1 - 2 * (jnp.arange(N_SEQ, dtype=jnp.int32) % 2)
    shift = shift.at[half_dp - 1].set(sign * (MEAN_KEPT - 1))
    counts = jnp.concatenate([MEAN_KEPT + shift, MEAN_KEPT - shift], axis=0).astype(jnp.int32)
    keys = jax.random.split(jax.random.fold_in(key, 701), N_DP * N_SEQ)
    picks = jax.vmap(lambda one: jax.random.permutation(one, TOK_DEV)[:CAPACITY])(keys)
    picks = picks.reshape(N_DP, N_SEQ, CAPACITY).astype(jnp.int32)
    slot_ids = jnp.arange(CAPACITY, dtype=jnp.int32)
    live = slot_ids[None, None, :] < counts[:, :, None]
    ordered = jnp.sort(jnp.where(live, picks, TOK_DEV + slot_ids[None, None, :]), axis=-1)
    rows = jnp.where(live, ordered, 0).astype(jnp.int32)
    return (counts, rows)


def draw_counts(key, part):
    counts, rows = routing(key)
    return counts


def draw_kept_rows(key, part):
    counts, rows = routing(key)
    return rows


def block_levels(key, extent, shards, smallest, top_value):
    gain = 1.0
    for axis_at, blocks in shards:
        draws = jax.random.uniform(jax.random.fold_in(jax.random.fold_in(key, 6), axis_at), (blocks,), jnp.float32, smallest / len(shards), top_value / len(shards))
        gain = gain * jnp.repeat(jnp.exp(draws), extent[axis_at] // blocks).reshape((-1,) + (1,) * (len(extent) - 1 - axis_at))
    return gain


def scatter_about(stream_key, shape, scale, limit, shards=(), kind=jnp.bfloat16):
    array = jax.random.normal(stream_key, shape, jnp.float32) * scale
    if len(shards) > 0:
        array = block_levels(stream_key, shape, shards, -0.22, 0.18) * array
    return jnp.clip(array, min=-limit, max=limit).astype(kind)


def setup_inputs(seed: int = 0) -> dict:
    splits = jax.random.split(jax.random.key(seed), 9)
    return {
        "residual": scatter_about(splits[0], (TOKENS, WIDTH), 1.0, 6.0, ((0, 512),)),
        "queries": draw_queries(jax.random.fold_in(splits[8], 71), 0),
        "key_proj": draw_key_proj(jax.random.fold_in(splits[8], 71), 0),
        "value_proj": scatter_about(splits[3], (KEPT_SLOTS, WIDTH), 1.0, 6.0, ((0, 512),)),
        "out_grad": scatter_about(splits[4], (KEPT_SLOTS, WIDTH), 1.0, 6.0, ((0, 512),)),
        "router": scatter_about(splits[5], (WIDTH,), WIDTH ** -0.5, 0.125, (), jnp.float32),
        "counts": draw_counts(jax.random.fold_in(splits[8], 71), 0),
        "kept_rows": draw_kept_rows(jax.random.fold_in(splits[8], 71), 0),
    }


def attend_rows(q_rows, k_rows, v_rows, x_rows, g_rows, router, q_pos, q_live, k_pos, k_live):
    width = q_rows.shape[1]
    head_dim = width // HEADS
    inv_scale = 1.0 / math.sqrt(head_dim)
    qh = q_rows.astype(jnp.float32).reshape(-1, HEADS, head_dim)
    kh = k_rows.astype(jnp.float32).reshape(-1, HEADS, head_dim)
    vh = v_rows.astype(jnp.float32).reshape(-1, HEADS, head_dim)
    scores = jnp.einsum('qhd,khd->hqk', qh, kh) * inv_scale
    allowed = k_live[None, :] & (k_pos[None, :] <= q_pos[:, None])
    scores = jnp.where(allowed[None], scores, -1e+30)
    probs = jax.nn.softmax(scores, axis=-1)
    probs_low = probs.astype(jnp.bfloat16).astype(jnp.float32)
    attended = jnp.einsum('hqk,khd->qhd', probs_low, vh).reshape(-1, width)
    x_wide = x_rows.astype(jnp.float32)
    gate = jax.nn.sigmoid(jnp.dot(x_wide, router, precision=lax.Precision.HIGHEST))
    mixed = x_wide + gate[:, None] * attended
    live_f = q_live.astype(jnp.float32)
    g_wide = g_rows.astype(jnp.float32)
    d_att = ((gate * live_f)[:, None] * g_wide).astype(jnp.bfloat16).astype(jnp.float32)
    d_gate = lax.optimization_barrier(jnp.sum(g_wide * attended, axis=-1))
    d_logit = d_gate * gate * (1.0 - gate) * live_f
    d_router = jnp.dot(d_logit, x_wide, precision=lax.Precision.HIGHEST)
    dah = d_att.reshape(-1, HEADS, head_dim)
    d_probs = jnp.einsum('qhd,khd->hqk', dah, vh)
    d_scores = probs * (d_probs - lax.optimization_barrier(jnp.sum(probs * d_probs, axis=-1, keepdims=True))) * inv_scale
    d_scores = d_scores.astype(jnp.bfloat16).astype(jnp.float32)
    d_query = jnp.einsum('hqk,khd->qhd', d_scores, kh).reshape(-1, width)
    d_key = jnp.einsum('hqk,qhd->khd', d_scores, qh).reshape(-1, width)
    d_value = jnp.einsum('hqk,qhd->khd', probs_low, dah).reshape(-1, width)
    return (mixed, d_query, d_key, d_value, d_router)

def reference(residual, queries, key_proj, value_proj, out_grad, router, counts, kept_rows):

    def one_sequence(items):
        res_seq, q_seq, k_seq, v_seq, g_seq, seq_counts, seq_rows = items
        slot_ids = jnp.arange(CAPACITY, dtype=jnp.int32)
        live = (slot_ids[None, :] < seq_counts[:, None]).reshape(-1)
        pos = (jnp.arange(N_SEQ, dtype=jnp.int32)[:, None] * TOK_DEV + seq_rows).reshape(-1).astype(jnp.int32)
        x_rows = jnp.take(res_seq, pos, axis=0)
        mixed, d_query, d_key, d_value, d_router = attend_rows(q_seq, k_seq, v_seq, x_rows, g_seq, router, pos, live, pos, live)
        target = jnp.where(live, pos, SEQ_LEN).astype(jnp.int32)
        out_seq = res_seq.at[target].set(mixed.astype(jnp.bfloat16), mode='drop')
        q_out = jnp.where(live[:, None], d_query, 0.0).astype(jnp.bfloat16)
        k_out = jnp.where(live[:, None], d_key, 0.0).astype(jnp.bfloat16)
        v_out = jnp.where(live[:, None], d_value, 0.0).astype(jnp.bfloat16)
        return (out_seq, q_out, k_out, v_out, d_router)

    def per_seq(a):
        return a.reshape(N_DP, -1, a.shape[1])
    results = lax.map(one_sequence, (per_seq(residual), per_seq(queries), per_seq(key_proj), per_seq(value_proj), per_seq(out_grad), counts, kept_rows))
    out_full = results[0].reshape(TOKENS, WIDTH)
    lists = [r.reshape(KEPT_SLOTS, WIDTH) for r in results[1:4]]
    return (out_full, lists[0], lists[1], lists[2], lax.optimization_barrier(jnp.sum(results[4], axis=0)))
```

```python
import functools
import math

import jax
import jax.numpy as jnp
from jax import lax
from jax.experimental import pallas as pl
from jax.experimental.pallas import tpu as pltpu
from jax.sharding import Mesh
from jax.sharding import PartitionSpec as P

HEADS = 16
LANES = 128
CORES = 2
MIB = 1024 * 1024
VMEM = pl.BlockSpec(memory_space=pltpu.VMEM)
SMEM = pl.BlockSpec(memory_space=pltpu.SMEM)


def flipped(row):
    n = row.shape[1]
    down = lax.broadcasted_iota(jnp.int32, (n, n), 0)
    along = lax.broadcasted_iota(jnp.int32, (n, n), 1)
    return jnp.sum(jnp.where(down == along, row, 0.0), axis=1, keepdims=True)


def prep_kernel(place, counts, rows, residual, queries, keys, values, grads, router, sent, picked, gates):
    slots, width = queries.shape
    groups = sent.shape[0]
    part = width // groups
    tokens = residual.shape[0]
    own = rows[0, pl.ds(place[1], 1), :].astype(jnp.float32)
    slot = lax.broadcasted_iota(jnp.int32, (slots, 1), 0)
    live = slot < counts[place[0], place[1]]
    token = lax.broadcasted_iota(jnp.int32, (slots, tokens), 1).astype(jnp.float32)
    pick = (flipped(own) == token).astype(jnp.bfloat16)
    x = jnp.dot(pick, residual[...], preferred_element_type=jnp.float32)
    picked[...] = x.astype(jnp.bfloat16)
    gate = jax.nn.sigmoid(jnp.sum(x * router[...], axis=1, keepdims=True))
    gates[...] = jnp.broadcast_to(gate, gates.shape)
    d_att = (jnp.where(live, gate, 0.0) * grads[...].astype(jnp.float32)).astype(jnp.bfloat16)
    for group in range(groups):
        columns = slice(group * part, (group + 1) * part)
        sent[group, 0] = queries[:, columns]
        sent[group, 1] = keys[:, columns]
        sent[group, 2] = values[:, columns]
        sent[group, 3] = d_att[:, columns]


def attend_kernel(place, counts, rows, got, sent, *, tok_dev):
    blocks, _, slots, part = got.shape
    n = blocks * slots
    spread = (
        lax.broadcasted_iota(jnp.int32, (slots, n), 1) % slots
        == lax.broadcasted_iota(jnp.int32, (slots, n), 0)
    ).astype(jnp.float32)
    tiled = jnp.dot(rows[0].astype(jnp.float32), spread, preferred_element_type=jnp.float32)
    along = lax.broadcasted_iota(jnp.int32, (1, n), 1)
    k_block, k_slot = along // slots, along % slots
    k_pos = jnp.zeros((1, n), jnp.float32)
    k_count = jnp.zeros((1, n), jnp.int32)
    for block in range(blocks):
        here = k_block == block
        k_pos = jnp.where(here, tiled[block : block + 1] + float(block * tok_dev), k_pos)
        k_count = jnp.where(here, counts[place[0], block], k_count)
    allowed = (k_pos <= flipped(k_pos)) & (k_slot < k_count)
    inv_scale = 1.0 / math.sqrt(LANES)
    mm = functools.partial(lax.dot_general, preferred_element_type=jnp.float32)
    for head in range(part // LANES):
        columns = slice(head * LANES, (head + 1) * LANES)
        q, k, v, da = (got[:, i, :, columns].reshape(n, LANES) for i in range(4))
        scores = mm(q, k, (((1,), (1,)), ((), ()))) * inv_scale
        scores = jnp.where(allowed, scores, -1e30)
        e = jnp.exp(scores - jnp.max(scores, axis=1, keepdims=True))
        probs = e * (1.0 / jnp.sum(e, axis=1, keepdims=True))
        low = probs.astype(jnp.bfloat16)
        att = mm(low, v, (((1,), (0,)), ((), ())))
        d_probs = mm(da, v, (((1,), (1,)), ((), ())))
        d_scores = probs * (d_probs - jnp.sum(probs * d_probs, axis=1, keepdims=True)) * inv_scale
        d_scores = d_scores.astype(jnp.bfloat16)
        dq = mm(d_scores, k, (((1,), (0,)), ((), ())))
        dk = mm(d_scores, q, (((0,), (0,)), ((), ())))
        dv = mm(low, da, (((0,), (0,)), ((), ())))
        for i, value in enumerate((att, dq, dk, dv)):
            sent[:, i, :, columns] = value.astype(jnp.bfloat16).reshape(blocks, slots, LANES)


def finish_kernel(
    place, counts, rows, got, residual, grads, picked, gates, block_out, d_queries, d_keys, d_values, d_router
):
    groups, _, slots, part = got.shape
    tokens, width = residual.shape
    count = counts[place[0], place[1]]
    live = lax.broadcasted_iota(jnp.int32, (slots, 1), 0) < count
    gate = gates[:, :1]
    d_gate = jnp.zeros((slots, 1), jnp.float32)
    for group in range(groups):
        columns = slice(group * part, (group + 1) * part)
        att = got[group, 0].astype(jnp.float32)
        d_gate += jnp.sum(grads[:, columns].astype(jnp.float32) * att, axis=1, keepdims=True)
    d_logit = jnp.where(live, d_gate * gate * (1.0 - gate), 0.0)
    x = picked[...].astype(jnp.float32)
    term = jnp.sum(d_logit * x, axis=0, keepdims=True)
    for k in range(width // LANES):
        piece = term[:, k * LANES : (k + 1) * LANES]
        d_router[:, k : k + 1, :] = jnp.broadcast_to(piece[None], (d_router.shape[0], 1, LANES))
    own = rows[0, pl.ds(place[1], 1), :].astype(jnp.float32)
    along = lax.broadcasted_iota(jnp.int32, (1, slots), 1)
    own = jnp.where(along < count, own, -1.0)
    token = lax.broadcasted_iota(jnp.int32, (tokens, slots), 0).astype(jnp.float32)
    put = (token == own).astype(jnp.float32)
    hit = jnp.sum(put, axis=1, keepdims=True) > 0.0
    put = put.astype(jnp.bfloat16)
    for group in range(groups):
        columns = slice(group * part, (group + 1) * part)
        att = got[group, 0].astype(jnp.float32)
        mixed = (x[:, columns] + gate * att).astype(jnp.bfloat16)
        moved = jnp.dot(put, mixed, preferred_element_type=jnp.float32).astype(jnp.bfloat16)
        block_out[:, columns] = jnp.where(hit, moved, residual[:, columns])
        for i, out in enumerate((d_queries, d_keys, d_values)):
            out[:, columns] = jnp.where(live, got[group, 1 + i], jnp.zeros((), jnp.bfloat16))


def call(kernel, out_shape, place, counts, rows, *operands, flops):
    slots = rows.shape[2]
    blocks = rows.shape[1]

    def whole(array):
        return pl.BlockSpec(array.shape, lambda i, *_: (0,) * len(array.shape))

    outs = jax.tree.map(whole, out_shape)
    moved = sum(o.size * o.dtype.itemsize for o in (*operands, *jax.tree.leaves(out_shape)))
    return pl.pallas_call(
        kernel,
        out_shape=out_shape,
        grid_spec=pltpu.PrefetchScalarGridSpec(
            num_scalar_prefetch=2,
            grid=(1,),
            in_specs=[pl.BlockSpec((1, blocks, slots), lambda i, place, counts: (place[0], 0, 0))]
            + [whole(o) for o in operands],
            out_specs=outs,
        ),
        compiler_params=pltpu.CompilerParams(vmem_limit_bytes=40 * MIB),
        cost_estimate=pl.CostEstimate(flops=flops, bytes_accessed=moved, transcendentals=0),
    )(place, counts, rows, *operands)


def shards(residual, queries, keys, values, grads, router, counts, rows, *, sizes):
    n_y, n_z, n_c, groups = sizes
    tok_dev, width = residual.shape
    slots = queries.shape[0]
    part = width // groups
    bf16, f32 = jnp.bfloat16, jnp.float32
    dp_index = (lax.axis_index("y") * n_z + lax.axis_index("z")) * n_c + lax.axis_index("c")
    place = jnp.stack([dp_index, lax.axis_index("x")]).astype(jnp.int32)
    shape = jax.ShapeDtypeStruct
    packed = shape((groups, 4, slots, part), bf16)
    sent, picked, gates = call(
        prep_kernel,
        (packed, shape((slots, width), bf16), shape((slots, LANES), f32)),
        place, counts, rows, residual, queries, keys, values, grads, router.reshape(1, width),
        flops=2 * slots * tok_dev * width,
    )
    got = lax.all_to_all(sent, "x", 0, 0)
    back = call(
        functools.partial(attend_kernel, tok_dev=tok_dev),
        packed, place, counts, rows, got,
        flops=12 * (groups * slots) ** 2 * part,
    )
    back = lax.all_to_all(back, "x", 0, 0)
    wide = shape((slots, width), bf16)
    block_out, d_queries, d_keys, d_values, term = call(
        finish_kernel,
        (shape((tok_dev, width), bf16), wide, wide, wide, shape((n_c * groups, width // LANES, LANES), f32)),
        place, counts, rows, back, residual, grads, picked, gates,
        flops=2 * slots * tok_dev * width,
    )
    total = jnp.sum(lax.all_to_all(term, ("c", "x"), 0, 0), axis=0)
    for axis, size in (("y", n_y), ("z", n_z)):
        copies = jnp.broadcast_to(total[None], (size, *total.shape))
        total = jnp.sum(lax.all_to_all(copies, axis, 0, 0), axis=0)
    return block_out, d_queries, d_keys, d_values, total.reshape(width)


def split_dp(size):
    chips = size // CORES
    z = 2 ** (int(math.log2(chips)) // 2)
    return chips // z, z, CORES


def solution(mesh):
    sizes = (*split_dp(mesh.shape["dp"]), mesh.shape["seq"])
    fine = Mesh(mesh.devices.reshape(sizes), ("y", "z", "c", "x"))
    split = P(("y", "z", "c", "x"), None)
    return jax.shard_map(
        functools.partial(shards, sizes=sizes),
        mesh=fine,
        in_specs=(split,) * 5 + (P(),) * 3,
        out_specs=(split,) * 4 + (P(),),
        check_vma=False,
    )
```

```python
import functools
import math

import jax
import jax.numpy as jnp
from jax import lax
from jax.experimental import pallas as pl
from jax.experimental.pallas import tpu as pltpu
from jax.sharding import Mesh
from jax.sharding import PartitionSpec as P

HEADS = 16
LANES = 128
CORES = 2
MIB = 1024 * 1024
ORDER = (("y", lambda s: s[0]), (("c", "x"), lambda s: s[2] * s[3]), ("z", lambda s: s[1]))
VMEM = pl.BlockSpec(memory_space=pltpu.VMEM)
ANY = pl.BlockSpec(memory_space=pl.ANY)
HBM = pl.BlockSpec(memory_space=pltpu.HBM)


def sequence_index(sizes):
    _, n_z, n_c, _ = sizes
    return (lax.axis_index("y") * n_z + lax.axis_index("z")) * n_c + lax.axis_index("c")


def column(table, index):
    lane = lax.broadcasted_iota(jnp.int32, table.shape, 1)
    return jnp.sum(jnp.where(lane == index, table, 0), axis=1, keepdims=True).astype(jnp.float32)


def prep_kernel(
    residual, queries, keys, values, grads, router, counts, rows, sent, picked, marks,
    residual_v, grads_v, straight_v, router_v, counts_v, rows_v, d_att_v, sems, *, sizes,
):
    slots, width = queries.shape
    groups, _, _, part = sent.shape
    tokens = residual.shape[0]
    dp_index, block_index = sequence_index(sizes), lax.axis_index("x")

    def fetch(source, target, i):
        copy = pltpu.make_async_copy(source, target, sems.at[i])
        copy.start()
        return copy

    small = [fetch(rows.at[block_index], rows_v, 0), fetch(counts, counts_v, 1), fetch(router, router_v, 2)]
    wide = [fetch(residual, residual_v, 3), fetch(grads, grads_v, 4)]
    pieces = [pl.ds(group * part, part) for group in range(groups)]
    straight = [fetch(array, straight_v.at[i], 5 + i) for i, array in enumerate((queries, keys, values))]
    for copy in small:
        copy.wait()
    count = column(counts_v[...], dp_index)
    own_block = lax.broadcasted_iota(jnp.int32, count.shape, 0) == block_index
    count = jnp.sum(jnp.where(own_block, count, 0.0), axis=0, keepdims=True)
    live = lax.broadcasted_iota(jnp.int32, (slots, 1), 0).astype(jnp.float32) < count
    token = lax.broadcasted_iota(jnp.int32, (slots, tokens), 1).astype(jnp.float32)
    pick = (column(rows_v[...], dp_index) == token).astype(jnp.bfloat16)
    wide[0].wait()
    x = jnp.dot(pick, residual_v[...], preferred_element_type=jnp.float32)
    picked[...] = x.astype(jnp.bfloat16)
    gate = jax.nn.sigmoid(jnp.sum(x * router_v[...], axis=1, keepdims=True))
    lane = lax.broadcasted_iota(jnp.int32, marks.shape, 1)
    marks[...] = jnp.where(lane == 0, gate, live.astype(jnp.float32))
    copies = []
    for i, copy in enumerate(straight):
        copy.wait()
        for group in range(groups):
            copies.append(fetch(straight_v.at[i, :, pieces[group]], sent.at[group, i], 8 + 4 * group + i))
    wide[1].wait()
    gate = jnp.where(live, gate, 0.0)
    for group in range(groups):
        columns = slice(group * part, (group + 1) * part)
        d_att_v[group] = (gate * grads_v[:, columns].astype(jnp.float32)).astype(jnp.bfloat16)
        copies.append(fetch(d_att_v.at[group], sent.at[group, 3], 11 + 4 * group))
    for copy in copies:
        copy.wait()


def mask_kernel(counts, rows, mask, places, *, sizes, tok_dev):
    blocks, slots, _ = rows.shape
    n = blocks * slots
    dp_index, block_index = sequence_index(sizes), lax.axis_index("x")
    row = column(rows[...].reshape(n, rows.shape[2]), dp_index)
    count = column(counts[...], dp_index)
    slot = lax.broadcasted_iota(jnp.int32, (n, 1), 0)
    block = slot // slots
    counted = jnp.zeros((n, 1), jnp.float32)
    for b in range(blocks):
        counted = jnp.where(block == b, count[b : b + 1], counted)
    live = (slot % slots).astype(jnp.float32) < counted
    position = row + (block * tok_dev).astype(jnp.float32)
    down = lax.broadcasted_iota(jnp.int32, (n, n), 0)
    along = lax.broadcasted_iota(jnp.int32, (n, n), 1)
    seen = jnp.where(live, position, float(blocks * tok_dev))
    seen = jnp.sum(jnp.where(down == along, seen, 0.0), axis=0, keepdims=True)
    mask[...] = (seen <= position).astype(jnp.float32)
    own = jnp.where(live & (block == block_index), row + 1.0, 0.0)
    down = lax.broadcasted_iota(jnp.int32, (n, LANES), 0) % slots
    along = lax.broadcasted_iota(jnp.int32, (n, LANES), 1)
    own = jnp.sum(jnp.where(down == along, own, 0.0), axis=0, keepdims=True) - 1.0
    places[...] = jnp.broadcast_to(own, places.shape)


def forward_kernel(got, mask, attended, probs, dots):
    blocks, _, slots, part = got.shape
    n = blocks * slots
    allowed = mask[...] > 0.0
    inv_scale = 1.0 / math.sqrt(LANES)
    mm = functools.partial(lax.dot_general, preferred_element_type=jnp.float32)
    dot = jnp.zeros((n, LANES), jnp.float32)
    for head in range(part // LANES):
        columns = slice(head * LANES, (head + 1) * LANES)
        q, k, v, da = (got[:, i, :, columns].reshape(n, LANES) for i in range(4))
        scores = mm(q, k, (((1,), (1,)), ((), ()))) * inv_scale
        scores = jnp.where(allowed, scores, -1e30)
        e = jnp.exp(scores - jnp.max(scores, axis=1, keepdims=True))
        weights = e * (1.0 / jnp.sum(e, axis=1, keepdims=True))
        probs[head] = weights
        att = mm(weights.astype(jnp.bfloat16), v, (((1,), (0,)), ((), ())))
        attended[:, columns] = att.astype(jnp.bfloat16)
        dot += att * da.astype(jnp.float32)
    ones = jnp.ones((8, LANES), jnp.float32)
    dot = mm(ones, dot, (((1,), (1,)), ((), ())), precision=lax.Precision.HIGHEST)
    dots[...] = jnp.broadcast_to(dot[None], dots.shape)


def backward_kernel(got, attended, probs, *refs):
    blocks, _, slots, part = got.shape
    *outs, held, sems = refs
    n = blocks * slots
    inv_scale = 1.0 / math.sqrt(LANES)
    mm = functools.partial(lax.dot_general, preferred_element_type=jnp.float32)
    for head in range(part // LANES):
        columns = slice(head * LANES, (head + 1) * LANES)
        q, k, v, da = (got[:, i, :, columns].reshape(n, LANES) for i in range(4))
        weights = probs[head]
        d_probs = mm(da, v, (((1,), (1,)), ((), ())))
        d_scores = weights * (d_probs - jnp.sum(weights * d_probs, axis=1, keepdims=True)) * inv_scale
        d_scores = d_scores.astype(jnp.bfloat16)
        dq = mm(d_scores, k, (((1,), (0,)), ((), ())))
        dk = mm(d_scores, q, (((0,), (0,)), ((), ())))
        dv = mm(weights.astype(jnp.bfloat16), da, (((0,), (0,)), ((), ())))
        for i, value in enumerate((dq, dk, dv)):
            held[:, i, :, columns] = value.astype(jnp.bfloat16).reshape(blocks, slots, LANES)
    copies = []
    for distance, out in enumerate(outs):
        block = lax.rem(lax.axis_index("x") + distance, blocks)
        first = pl.multiple_of(block * slots, slots)
        copies.append(pltpu.make_async_copy(attended.at[pl.ds(first, slots), :], out.at[0], sems.at[2 * distance]))
        copies.append(pltpu.make_async_copy(held.at[block], out.at[pl.ds(1, 3)], sems.at[2 * distance + 1]))
    for copy in copies:
        copy.start()
    for copy in copies:
        copy.wait()


def router_kernel(dots, picked, marks, after, d_router):
    slots, width = picked.shape
    n = dots.shape[2]
    dot = jnp.sum(dots[...], axis=0)[0:1]
    first = lax.axis_index("x") * slots
    mine = lax.broadcasted_iota(jnp.int32, (slots, n), 0) + first
    dot = jnp.where(mine == lax.broadcasted_iota(jnp.int32, (slots, n), 1), dot, 0.0)
    d_logit = jnp.sum(dot, axis=1, keepdims=True) * (1.0 - marks[:, 0:1])
    term = jnp.sum(d_logit * picked[...].astype(jnp.float32), axis=0, keepdims=True)
    d_router[...] = jnp.broadcast_to(term[None], d_router.shape)


def finish_kernel(*refs):
    groups = lax.axis_size("x")
    got = refs[:groups]
    residual, picked, marks, places, block_out, d_queries, d_keys, d_values, block_v, lists_v, sems = refs[groups:]
    _, slots, part = got[0].shape
    tokens, width = residual.shape
    gate, live = marks[:, 0:1], marks[:, 1:2] > 0.0
    own = places[0:1, :slots]
    token = lax.broadcasted_iota(jnp.int32, (tokens, slots), 0).astype(jnp.float32)
    put = (token == own).astype(jnp.float32)
    hit = jnp.sum(put, axis=1, keepdims=True) > 0.0
    put = put.astype(jnp.bfloat16)
    copies = []

    def store(source, target):
        copy = pltpu.make_async_copy(source, target, sems.at[len(copies)])
        copy.start()
        copies.append(copy)

    for distance in range(groups):
        group = lax.rem(lax.axis_index("x") + (groups - distance), groups)
        columns = pl.ds(pl.multiple_of(group * part, part), part)
        for i, out in enumerate((d_queries, d_keys, d_values)):
            lists_v[i, distance] = jnp.where(live, got[distance][1 + i], jnp.zeros((), jnp.bfloat16))
            store(lists_v.at[i, distance], out.at[:, columns])
        att = got[distance][0].astype(jnp.float32)
        mixed = (picked[:, columns].astype(jnp.float32) + gate * att).astype(jnp.bfloat16)
        moved = jnp.dot(put, mixed, preferred_element_type=jnp.float32).astype(jnp.bfloat16)
        block_v[distance] = jnp.where(hit, moved, residual[:, columns])
        store(block_v.at[distance], block_out.at[:, columns])
    for copy in copies:
        copy.wait()


def call(kernel, out_shape, *operands, in_specs, out_specs, scratch_shapes=(), flops):
    outs = out_shape if isinstance(out_shape, tuple) else (out_shape,)
    moved = sum(math.prod(o.shape) * o.dtype.itemsize for o in (*operands, *outs))
    return pl.pallas_call(
        kernel,
        out_shape=out_shape,
        in_specs=in_specs,
        out_specs=out_specs,
        scratch_shapes=scratch_shapes,
        compiler_params=pltpu.CompilerParams(vmem_limit_bytes=24 * MIB),
        cost_estimate=pl.CostEstimate(flops=flops, bytes_accessed=moved, transcendentals=0),
    )(*operands)


def shards(residual, queries, keys, values, grads, router, counts, rows, *, sizes):
    n_y, n_z, n_c, groups = sizes
    tok_dev, width = residual.shape
    slots = queries.shape[0]
    part = width // groups
    bf16, f32 = jnp.bfloat16, jnp.float32
    shape = jax.ShapeDtypeStruct
    packed = shape((groups, 4, slots, part), bf16)
    wide = shape((slots, width), bf16)
    dma = pltpu.SemaphoreType.DMA
    pin = functools.partial(pltpu.with_memory_space_constraint, memory_space=pltpu.HBM)
    router = router.reshape(1, width)
    counts, rows = counts.T, jnp.transpose(rows, (1, 2, 0))
    sent, picked, marks = call(
        functools.partial(prep_kernel, sizes=sizes),
        (pltpu.HBM(packed.shape, bf16), wide, shape((slots, LANES), f32)),
        *(pin(a) for a in (residual, queries, keys, values, grads, router, counts, rows)),
        in_specs=[HBM] * 8,
        out_specs=(HBM, VMEM, VMEM),
        scratch_shapes=[
            pltpu.VMEM((tok_dev, width), bf16),
            pltpu.VMEM((slots, width), bf16),
            pltpu.VMEM((3, slots, width), bf16),
            pltpu.VMEM((1, width), f32),
            pltpu.VMEM(counts.shape, jnp.int32),
            pltpu.VMEM(rows.shape[1:], jnp.int32),
            pltpu.VMEM((groups, slots, part), bf16),
            dma((8 + 4 * groups,)),
        ],
        flops=2 * slots * tok_dev * width,
    )

    def passed(array, distance):
        return lax.ppermute(array, "x", [(i, (i + distance) % groups) for i in range(groups)])

    got = lax.all_to_all(sent, "x", 0, 0)
    n = groups * slots
    mask, places = call(
        functools.partial(mask_kernel, sizes=sizes, tok_dev=tok_dev),
        (shape((n, n), f32), shape((8, LANES), f32)),
        counts, rows,
        in_specs=[VMEM] * 2, out_specs=(VMEM,) * 2, flops=10 * n * n,
    )
    attended, probs, dots = call(
        forward_kernel,
        (shape((n, part), bf16), shape((part // LANES, n, n), f32), shape((groups, 8, n), f32)),
        got, mask,
        in_specs=[VMEM] * 2, out_specs=(VMEM,) * 3, flops=4 * n * n * part,
    )
    dots = lax.all_to_all(dots, "x", 0, 0)
    back = call(
        backward_kernel, (pltpu.HBM((4, slots, part), bf16),) * groups, got, attended, probs,
        in_specs=[VMEM] * 3, out_specs=(HBM,) * groups,
        scratch_shapes=[pltpu.VMEM((groups, 3, slots, part), bf16), dma((2 * groups,))],
        flops=8 * n * n * part,
    )
    back = [back[0]] + [passed(back[d], d) for d in range(1, groups)]
    term = call(
        router_kernel, shape((ORDER[0][1](sizes), 1, width), f32), dots, picked, marks, pin(back[0]),
        in_specs=[VMEM] * 3 + [HBM], out_specs=VMEM, flops=4 * n * width,
    )
    total = jnp.sum(lax.all_to_all(term, ORDER[0][0], 0, 0), axis=0)
    for axes, size in ORDER[1:]:
        copies = jnp.broadcast_to(total[None], (size(sizes), 1, width))
        total = jnp.sum(lax.all_to_all(copies, axes, 0, 0), axis=0)
    block_out, d_queries, d_keys, d_values = call(
        finish_kernel,
        (shape((tok_dev, width), bf16), wide, wide, wide),
        *back, residual, picked, marks, places,
        in_specs=[VMEM] * (groups + 4),
        out_specs=(ANY,) * 4,
        scratch_shapes=[
            pltpu.VMEM((groups, tok_dev, part), bf16),
            pltpu.VMEM((3, groups, slots, part), bf16),
            dma((4 * groups,)),
        ],
        flops=2 * slots * tok_dev * width,
    )
    return block_out, d_queries, d_keys, d_values, total.reshape(width)


def split_dp(size):
    chips = size // CORES
    z = 2 ** (int(math.log2(chips)) // 2)
    return chips // z, z, CORES


def solution(mesh):
    sizes = (*split_dp(mesh.shape["dp"]), mesh.shape["seq"])
    fine = Mesh(mesh.devices.reshape(sizes), ("y", "z", "c", "x"))
    split = P(("y", "z", "c", "x"), None)
    return jax.shard_map(
        functools.partial(shards, sizes=sizes),
        mesh=fine,
        in_specs=(split,) * 5 + (P(),) * 3,
        out_specs=(split,) * 4 + (P(),),
        check_vma=False,
    )
```

```python
import functools
import math

import jax
import jax.numpy as jnp
from jax import lax
from jax.experimental import pallas as pl
from jax.experimental.pallas import tpu as pltpu
from jax.sharding import Mesh
from jax.sharding import PartitionSpec as P

HEADS = 16
LANES = 128
CORES = 2
MIB = 1024 * 1024
ORDER = (("z", lambda s: s[1]), (("c", "x"), lambda s: s[2] * s[3]), ("y", lambda s: s[0]))
VMEM = pl.BlockSpec(memory_space=pltpu.VMEM)
ANY = pl.BlockSpec(memory_space=pl.ANY)
HBM = pl.BlockSpec(memory_space=pltpu.HBM)


def sequence_index(sizes):
    _, n_z, n_c, _ = sizes
    return (lax.axis_index("y") * n_z + lax.axis_index("z")) * n_c + lax.axis_index("c")


def column(table, index):
    lane = lax.broadcasted_iota(jnp.int32, table.shape, 1)
    return jnp.sum(jnp.where(lane == index, table, 0), axis=1, keepdims=True).astype(jnp.float32)


def prep_kernel(
    residual, queries, keys, values, grads, router, counts, rows, sent, picked, marks,
    residual_v, grads_v, straight_v, router_v, counts_v, rows_v, d_att_v, sems, *, sizes,
):
    slots, width = queries.shape
    groups, _, _, part = sent.shape
    tokens = residual.shape[0]
    dp_index, block_index = sequence_index(sizes), lax.axis_index("x")

    def fetch(source, target, i):
        copy = pltpu.make_async_copy(source, target, sems.at[i])
        copy.start()
        return copy

    small = [fetch(rows.at[block_index], rows_v, 0), fetch(counts, counts_v, 1), fetch(router, router_v, 2)]
    pieces = [pl.ds(group * part, part) for group in range(groups)]
    wide = [fetch(residual.at[:, p], residual_v.at[:, p], 3 + i) for i, p in enumerate(pieces)]
    base = 3 + groups
    grads_copy = fetch(grads, grads_v, base)
    straight = [fetch(array, straight_v.at[i], base + 1 + i) for i, array in enumerate((queries, keys, values))]
    base += 4
    for copy in small:
        copy.wait()
    count = column(counts_v[...], dp_index)
    own_block = lax.broadcasted_iota(jnp.int32, count.shape, 0) == block_index
    count = jnp.sum(jnp.where(own_block, count, 0.0), axis=0, keepdims=True)
    live = lax.broadcasted_iota(jnp.int32, (slots, 1), 0).astype(jnp.float32) < count
    token = lax.broadcasted_iota(jnp.int32, (slots, tokens), 1).astype(jnp.float32)
    pick = (column(rows_v[...], dp_index) == token).astype(jnp.bfloat16)
    logit = jnp.zeros((slots, part), jnp.float32)
    for copy, p in zip(wide, pieces):
        copy.wait()
        x = jnp.dot(pick, residual_v[:, p], preferred_element_type=jnp.float32)
        picked[:, p] = x.astype(jnp.bfloat16)
        logit += x * router_v[:, p]
    gate = jax.nn.sigmoid(jnp.sum(logit, axis=1, keepdims=True))
    lane = lax.broadcasted_iota(jnp.int32, marks.shape, 1)
    marks[...] = jnp.where(lane == 0, gate, live.astype(jnp.float32))
    copies = []
    for i, copy in enumerate(straight):
        copy.wait()
        for group in range(groups):
            copies.append(fetch(straight_v.at[i, :, pieces[group]], sent.at[group, i], base + 4 * group + i))
    grads_copy.wait()
    gate = jnp.where(live, gate, 0.0)
    for group in range(groups):
        columns = slice(group * part, (group + 1) * part)
        d_att_v[group] = (gate * grads_v[:, columns].astype(jnp.float32)).astype(jnp.bfloat16)
        copies.append(fetch(d_att_v.at[group], sent.at[group, 3], base + 4 * group + 3))
    for copy in copies:
        copy.wait()


def places_kernel(counts, rows, places, *, sizes, tok_dev):
    blocks, slots, _ = rows.shape
    n = blocks * slots
    dp_index, block_index = sequence_index(sizes), lax.axis_index("x")
    row = column(rows[...].reshape(n, rows.shape[2]), dp_index)
    count = column(counts[...], dp_index)
    slot = lax.broadcasted_iota(jnp.int32, (n, 1), 0)
    block = slot // slots
    counted = jnp.zeros((n, 1), jnp.float32)
    for b in range(blocks):
        counted = jnp.where(block == b, count[b : b + 1], counted)
    live = (slot % slots).astype(jnp.float32) < counted
    position = row + (block * tok_dev).astype(jnp.float32)
    down = lax.broadcasted_iota(jnp.int32, (n, n), 0)
    along = lax.broadcasted_iota(jnp.int32, (n, n), 1)
    seen = jnp.where(live, position, float(blocks * tok_dev))
    places[0:1, :] = jnp.sum(jnp.where(down == along, position, 0.0), axis=0, keepdims=True)
    places[1:2, :] = jnp.sum(jnp.where(down == along, seen, 0.0), axis=0, keepdims=True)
    own = jnp.where(live & (block == block_index), row + 1.0, 0.0)
    own = jnp.sum(jnp.where(down % slots == along % slots, own, 0.0), axis=0, keepdims=True) - 1.0
    places[2:3, :] = own


def forward_kernel(got, places, probs, d_probs, dots):
    blocks, _, slots, part = got.shape
    n = blocks * slots
    down = lax.broadcasted_iota(jnp.int32, (n, n), 0)
    along = lax.broadcasted_iota(jnp.int32, (n, n), 1)
    seen = jnp.sum(jnp.where(down == along, places[1:2, :], 0.0), axis=1, keepdims=True)
    allowed = seen <= places[0:1, :]
    inv_scale = 1.0 / math.sqrt(LANES)
    mm = functools.partial(lax.dot_general, preferred_element_type=jnp.float32)
    dot = jnp.zeros((1, n), jnp.float32)
    for head in range(part // LANES):
        columns = slice(head * LANES, (head + 1) * LANES)
        q, k, v, da = (got[:, i, :, columns].reshape(n, LANES) for i in range(4))
        scores = mm(k, q, (((1,), (1,)), ((), ()))) * inv_scale
        scores = jnp.where(allowed, scores, -1e30)
        e = jnp.exp(scores - jnp.max(scores, axis=0, keepdims=True))
        weights = e * (1.0 / jnp.sum(e, axis=0, keepdims=True))
        probs[head] = weights
        grad = mm(v, da, (((1,), (1,)), ((), ())))
        d_probs[head] = grad
        dot += jnp.sum(weights.astype(jnp.bfloat16).astype(jnp.float32) * grad, axis=0, keepdims=True)
    dots[...] = jnp.broadcast_to(dot[None], dots.shape)


def backward_kernel(got, probs, d_probs, *refs):
    blocks, _, slots, part = got.shape
    *outs, held, sems = refs
    n = blocks * slots
    inv_scale = 1.0 / math.sqrt(LANES)
    mm = functools.partial(lax.dot_general, preferred_element_type=jnp.float32)
    copies = []
    for head in range(part // LANES):
        columns = slice(head * LANES, (head + 1) * LANES)
        q, k, v, da = (got[:, i, :, columns].reshape(n, LANES) for i in range(4))
        weights, grad = probs[head], d_probs[head]
        d_scores = weights * (grad - jnp.sum(weights * grad, axis=0, keepdims=True)) * inv_scale
        d_scores, low = d_scores.astype(jnp.bfloat16), weights.astype(jnp.bfloat16)
        att = mm(low, v, (((0,), (0,)), ((), ())))
        dq = mm(d_scores, k, (((0,), (0,)), ((), ())))
        dk = mm(d_scores, q, (((1,), (0,)), ((), ())))
        dv = mm(low, da, (((1,), (0,)), ((), ())))
        for i, value in enumerate((att, dq, dk, dv)):
            held[:, i, :, columns] = value.astype(jnp.bfloat16).reshape(blocks, slots, LANES)
        if head % 2 == 1:
            done = pl.ds((head - 1) * LANES, 2 * LANES)
            for distance, out in enumerate(outs):
                block = lax.rem(lax.axis_index("x") + distance, blocks)
                copy = pltpu.make_async_copy(held.at[block, :, :, done], out.at[:, :, done], sems.at[len(copies)])
                copy.start()
                copies.append(copy)
    for copy in copies:
        copy.wait()


def router_kernel(dots, picked, marks, after, d_router, tile):
    slots, width = picked.shape
    n = dots.shape[2]
    dot = jnp.sum(dots[...], axis=0)[0:1]
    first = lax.axis_index("x") * slots
    mine = lax.broadcasted_iota(jnp.int32, (slots, n), 0) + first
    dot = jnp.where(mine == lax.broadcasted_iota(jnp.int32, (slots, n), 1), dot, 0.0)
    d_logit = jnp.sum(dot, axis=1, keepdims=True) * (1.0 - marks[:, 0:1])
    term = jnp.sum(d_logit * picked[...].astype(jnp.float32), axis=0, keepdims=True)
    for k in range(width // LANES):
        tile[k : k + 1, :] = term[:, k * LANES : (k + 1) * LANES]
    d_router[...] = jnp.broadcast_to(tile[...][None], d_router.shape)


def finish_kernel(*refs):
    groups = lax.axis_size("x")
    got = refs[:groups]
    residual, picked, marks, places, block_out, d_queries, d_keys, d_values, block_v, lists_v, sems = refs[groups:]
    _, slots, part = got[0].shape
    tokens, width = residual.shape
    gate, live = marks[:, 0:1], marks[:, 1:2] > 0.0
    own = places[2:3, :slots]
    token = lax.broadcasted_iota(jnp.int32, (tokens, slots), 0).astype(jnp.float32)
    put = (token == own).astype(jnp.float32)
    hit = jnp.sum(put, axis=1, keepdims=True) > 0.0
    put = put.astype(jnp.bfloat16)
    copies = []

    def store(source, target):
        copy = pltpu.make_async_copy(source, target, sems.at[len(copies)])
        copy.start()
        copies.append(copy)

    for distance in range(groups):
        group = lax.rem(lax.axis_index("x") + (groups - distance), groups)
        columns = pl.ds(pl.multiple_of(group * part, part), part)
        for i, out in enumerate((d_queries, d_keys, d_values)):
            lists_v[i, distance] = jnp.where(live, got[distance][1 + i], jnp.zeros((), jnp.bfloat16))
            store(lists_v.at[i, distance], out.at[:, columns])
        att = got[distance][0].astype(jnp.float32)
        mixed = (picked[:, columns].astype(jnp.float32) + gate * att).astype(jnp.bfloat16)
        moved = jnp.dot(put, mixed, preferred_element_type=jnp.float32).astype(jnp.bfloat16)
        block_v[distance] = jnp.where(hit, moved, residual[:, columns])
        store(block_v.at[distance], block_out.at[:, columns])
    for copy in copies:
        copy.wait()


def call(kernel, out_shape, *operands, in_specs, out_specs, scratch_shapes=(), flops):
    outs = out_shape if isinstance(out_shape, tuple) else (out_shape,)
    moved = sum(math.prod(o.shape) * o.dtype.itemsize for o in (*operands, *outs))
    return pl.pallas_call(
        kernel,
        out_shape=out_shape,
        in_specs=in_specs,
        out_specs=out_specs,
        scratch_shapes=scratch_shapes,
        compiler_params=pltpu.CompilerParams(vmem_limit_bytes=24 * MIB),
        cost_estimate=pl.CostEstimate(flops=flops, bytes_accessed=moved, transcendentals=0),
    )(*operands)


def shards(residual, queries, keys, values, grads, router, counts, rows, *, sizes):
    n_y, n_z, n_c, groups = sizes
    tok_dev, width = residual.shape
    slots = queries.shape[0]
    part = width // groups
    bf16, f32 = jnp.bfloat16, jnp.float32
    shape = jax.ShapeDtypeStruct
    packed = shape((groups, 4, slots, part), bf16)
    wide = shape((slots, width), bf16)
    dma = pltpu.SemaphoreType.DMA
    pin = functools.partial(pltpu.with_memory_space_constraint, memory_space=pltpu.HBM)
    router = router.reshape(1, width)
    counts, rows = counts.T, jnp.transpose(rows, (1, 2, 0))
    sent, picked, marks = call(
        functools.partial(prep_kernel, sizes=sizes),
        (pltpu.HBM(packed.shape, bf16), wide, shape((slots, LANES), f32)),
        *(pin(a) for a in (residual, queries, keys, values, grads, router, counts, rows)),
        in_specs=[HBM] * 8,
        out_specs=(HBM, VMEM, VMEM),
        scratch_shapes=[
            pltpu.VMEM((tok_dev, width), bf16),
            pltpu.VMEM((slots, width), bf16),
            pltpu.VMEM((3, slots, width), bf16),
            pltpu.VMEM((1, width), f32),
            pltpu.VMEM(counts.shape, jnp.int32),
            pltpu.VMEM(rows.shape[1:], jnp.int32),
            pltpu.VMEM((groups, slots, part), bf16),
            dma((7 + 5 * groups,)),
        ],
        flops=2 * slots * tok_dev * width,
    )

    def passed(array, distance):
        return lax.ppermute(array, "x", [(i, (i + distance) % groups) for i in range(groups)])

    got = lax.all_to_all(sent, "x", 0, 0)
    n = groups * slots
    places = call(
        functools.partial(places_kernel, sizes=sizes, tok_dev=tok_dev),
        shape((8, n), f32), counts, rows,
        in_specs=[VMEM] * 2, out_specs=VMEM, flops=10 * n * n,
    )
    square = shape((part // LANES, n, n), f32)
    probs, d_probs, dots = call(
        forward_kernel,
        (square, square, shape((groups, 8, n), f32)),
        got, places,
        in_specs=[VMEM] * 2, out_specs=(VMEM,) * 3, flops=4 * n * n * part,
    )
    dots = lax.all_to_all(dots, "x", 0, 0)
    back = call(
        backward_kernel, (pltpu.HBM((4, slots, part), bf16),) * groups, got, probs, d_probs,
        in_specs=[VMEM] * 3, out_specs=(HBM,) * groups,
        scratch_shapes=[pltpu.VMEM((groups, 4, slots, part), bf16), dma((part // LANES // 2 * groups,))],
        flops=8 * n * n * part,
    )
    back = [back[0]] + [passed(back[d], d) for d in range(1, groups)]
    term = call(
        router_kernel, shape((ORDER[0][1](sizes), width // LANES, LANES), f32), dots, picked, marks, pin(back[0]),
        in_specs=[VMEM] * 3 + [HBM], out_specs=VMEM,
        scratch_shapes=[pltpu.VMEM((width // LANES, LANES), f32)], flops=4 * n * width,
    )
    total = jnp.sum(lax.all_to_all(term, ORDER[0][0], 0, 0), axis=0)
    for axes, size in ORDER[1:]:
        copies = jnp.broadcast_to(total[None], (size(sizes), *total.shape))
        total = jnp.sum(lax.all_to_all(copies, axes, 0, 0), axis=0)
    block_out, d_queries, d_keys, d_values = call(
        finish_kernel,
        (shape((tok_dev, width), bf16), wide, wide, wide),
        *back, residual, picked, marks, places,
        in_specs=[VMEM] * (groups + 4),
        out_specs=(ANY,) * 4,
        scratch_shapes=[
            pltpu.VMEM((groups, tok_dev, part), bf16),
            pltpu.VMEM((3, groups, slots, part), bf16),
            dma((4 * groups,)),
        ],
        flops=2 * slots * tok_dev * width,
    )
    return block_out, d_queries, d_keys, d_values, total.reshape(width)


def split_dp(size):
    chips = size // CORES
    z = 2 ** (int(math.log2(chips)) // 2)
    return chips // z, z, CORES


def solution(mesh):
    sizes = (*split_dp(mesh.shape["dp"]), mesh.shape["seq"])
    fine = Mesh(mesh.devices.reshape(sizes), ("y", "z", "c", "x"))
    split = P(("y", "z", "c", "x"), None)
    return jax.shard_map(
        functools.partial(shards, sizes=sizes),
        mesh=fine,
        in_specs=(split,) * 5 + (P(),) * 3,
        out_specs=(split,) * 4 + (P(),),
        check_vma=False,
    )
```

```python
import functools
import math

import jax
import jax.numpy as jnp
from jax import lax
from jax.experimental import pallas as pl
from jax.experimental.pallas import tpu as pltpu
from jax.sharding import Mesh
from jax.sharding import PartitionSpec as P

HEADS = 16
LANES = 128
CORES = 2
MIB = 1024 * 1024
ORDER = (("z", lambda s: s[1]), (("c", "x"), lambda s: s[2] * s[3]), ("y", lambda s: s[0]))
VMEM = pl.BlockSpec(memory_space=pltpu.VMEM)
ANY = pl.BlockSpec(memory_space=pl.ANY)
HBM = pl.BlockSpec(memory_space=pltpu.HBM)


def sequence_index(sizes):
    _, n_z, n_c, _ = sizes
    return (lax.axis_index("y") * n_z + lax.axis_index("z")) * n_c + lax.axis_index("c")


def column(table, index):
    lane = lax.broadcasted_iota(jnp.int32, table.shape, 1)
    return jnp.sum(jnp.where(lane == index, table, 0), axis=1, keepdims=True).astype(jnp.float32)


def prep_kernel(
    residual, queries, keys, values, grads, router, counts, rows, sent, picked, marks,
    residual_v, grads_v, straight_v, router_v, counts_v, rows_v, d_att_v, sems, *, sizes,
):
    slots, width = queries.shape
    groups, _, _, part = sent.shape
    tokens = residual.shape[0]
    dp_index, block_index = sequence_index(sizes), lax.axis_index("x")

    def fetch(source, target, i):
        copy = pltpu.make_async_copy(source, target, sems.at[i])
        copy.start()
        return copy

    small = [fetch(rows.at[block_index], rows_v, 0), fetch(counts, counts_v, 1), fetch(router, router_v, 2)]
    pieces = [pl.ds(group * part, part) for group in range(groups)]
    base = 3 + groups
    straight = [fetch(array, straight_v.at[i], base + 1 + i) for i, array in enumerate((queries, keys, values))]
    wide = [fetch(residual.at[:, p], residual_v.at[:, p], 3 + i) for i, p in enumerate(pieces)]
    grads_copy = fetch(grads, grads_v, base)
    base += 4
    for copy in small:
        copy.wait()
    count = column(counts_v[...], dp_index)
    own_block = lax.broadcasted_iota(jnp.int32, count.shape, 0) == block_index
    count = jnp.sum(jnp.where(own_block, count, 0.0), axis=0, keepdims=True)
    live = lax.broadcasted_iota(jnp.int32, (slots, 1), 0).astype(jnp.float32) < count
    token = lax.broadcasted_iota(jnp.int32, (slots, tokens), 1).astype(jnp.float32)
    pick = (column(rows_v[...], dp_index) == token).astype(jnp.bfloat16)
    copies = []
    for i, copy in enumerate(straight):
        copy.wait()
        for group in range(groups):
            copies.append(fetch(straight_v.at[i, :, pieces[group]], sent.at[group, i], base + 4 * group + i))
    logit = jnp.zeros((slots, part), jnp.float32)
    for copy, p in zip(wide, pieces):
        copy.wait()
        x = jnp.dot(pick, residual_v[:, p], preferred_element_type=jnp.float32)
        picked[:, p] = x.astype(jnp.bfloat16)
        logit += x * router_v[:, p]
    gate = jax.nn.sigmoid(jnp.sum(logit, axis=1, keepdims=True))
    lane = lax.broadcasted_iota(jnp.int32, marks.shape, 1)
    marks[...] = jnp.where(lane == 0, gate, live.astype(jnp.float32))
    grads_copy.wait()
    gate = jnp.where(live, gate, 0.0)
    for group in range(groups):
        columns = slice(group * part, (group + 1) * part)
        d_att_v[group] = (gate * grads_v[:, columns].astype(jnp.float32)).astype(jnp.bfloat16)
        copies.append(fetch(d_att_v.at[group], sent.at[group, 3], base + 4 * group + 3))
    for copy in copies:
        copy.wait()


def places_kernel(counts, rows, places, *, sizes, tok_dev):
    blocks, slots, _ = rows.shape
    n = blocks * slots
    dp_index, block_index = sequence_index(sizes), lax.axis_index("x")
    row = column(rows[...].reshape(n, rows.shape[2]), dp_index)
    count = column(counts[...], dp_index)
    slot = lax.broadcasted_iota(jnp.int32, (n, 1), 0)
    block = slot // slots
    counted = jnp.zeros((n, 1), jnp.float32)
    for b in range(blocks):
        counted = jnp.where(block == b, count[b : b + 1], counted)
    live = (slot % slots).astype(jnp.float32) < counted
    position = row + (block * tok_dev).astype(jnp.float32)
    down = lax.broadcasted_iota(jnp.int32, (n, n), 0)
    along = lax.broadcasted_iota(jnp.int32, (n, n), 1)
    seen = jnp.where(live, position, float(blocks * tok_dev))
    places[0:1, :] = jnp.sum(jnp.where(down == along, position, 0.0), axis=0, keepdims=True)
    places[1:2, :] = jnp.sum(jnp.where(down == along, seen, 0.0), axis=0, keepdims=True)
    own = jnp.where(live & (block == block_index), row + 1.0, 0.0)
    own = jnp.sum(jnp.where(down % slots == along % slots, own, 0.0), axis=0, keepdims=True) - 1.0
    places[2:3, :] = own


def forward_kernel(got, places, probs, d_probs, dots):
    blocks, _, slots, part = got.shape
    n = blocks * slots
    down = lax.broadcasted_iota(jnp.int32, (n, n), 0)
    along = lax.broadcasted_iota(jnp.int32, (n, n), 1)
    seen = jnp.sum(jnp.where(down == along, places[1:2, :], 0.0), axis=1, keepdims=True)
    allowed = seen <= places[0:1, :]
    inv_scale = 1.0 / math.sqrt(LANES)
    mm = functools.partial(lax.dot_general, preferred_element_type=jnp.float32)
    dot = jnp.zeros((1, n), jnp.float32)
    for head in range(part // LANES):
        columns = slice(head * LANES, (head + 1) * LANES)
        q, k, v, da = (got[:, i, :, columns].reshape(n, LANES) for i in range(4))
        scores = mm(k, q, (((1,), (1,)), ((), ()))) * inv_scale
        scores = jnp.where(allowed, scores, -1e30)
        e = jnp.exp(scores - jnp.max(scores, axis=0, keepdims=True))
        weights = e * (1.0 / jnp.sum(e, axis=0, keepdims=True))
        probs[head] = weights
        grad = mm(v, da, (((1,), (1,)), ((), ())))
        d_probs[head] = grad
        dot += jnp.sum(weights.astype(jnp.bfloat16).astype(jnp.float32) * grad, axis=0, keepdims=True)
    dots[...] = jnp.broadcast_to(dot[None], dots.shape)


def backward_kernel(got, probs, d_probs, *refs):
    blocks, _, slots, part = got.shape
    *outs, held, sems = refs
    n = blocks * slots
    inv_scale = 1.0 / math.sqrt(LANES)
    mm = functools.partial(lax.dot_general, preferred_element_type=jnp.float32)
    copies = []
    for head in range(part // LANES):
        columns = slice(head * LANES, (head + 1) * LANES)
        q, k, v, da = (got[:, i, :, columns].reshape(n, LANES) for i in range(4))
        weights, grad = probs[head], d_probs[head]
        d_scores = weights * (grad - jnp.sum(weights * grad, axis=0, keepdims=True)) * inv_scale
        d_scores, low = d_scores.astype(jnp.bfloat16), weights.astype(jnp.bfloat16)
        att = mm(low, v, (((0,), (0,)), ((), ())))
        dq = mm(d_scores, k, (((0,), (0,)), ((), ())))
        dk = mm(d_scores, q, (((1,), (0,)), ((), ())))
        dv = mm(low, da, (((1,), (0,)), ((), ())))
        for i, value in enumerate((att, dq, dk, dv)):
            held[:, i, :, columns] = value.astype(jnp.bfloat16).reshape(blocks, slots, LANES)
        if head % 2 == 1:
            done = pl.ds((head - 1) * LANES, 2 * LANES)
            for distance, out in enumerate(outs):
                block = lax.rem(lax.axis_index("x") + distance, blocks)
                copy = pltpu.make_async_copy(held.at[block, :, :, done], out.at[:, :, done], sems.at[len(copies)])
                copy.start()
                copies.append(copy)
    for copy in copies:
        copy.wait()


def router_kernel(dots, picked, marks, after, d_router, tile):
    slots, width = picked.shape
    n = dots.shape[2]
    dot = jnp.sum(dots[...], axis=0)[0:1]
    first = lax.axis_index("x") * slots
    mine = lax.broadcasted_iota(jnp.int32, (slots, n), 0) + first
    dot = jnp.where(mine == lax.broadcasted_iota(jnp.int32, (slots, n), 1), dot, 0.0)
    d_logit = jnp.sum(dot, axis=1, keepdims=True) * (1.0 - marks[:, 0:1])
    term = jnp.sum(d_logit * picked[...].astype(jnp.float32), axis=0, keepdims=True)
    for k in range(width // LANES):
        tile[k : k + 1, :] = term[:, k * LANES : (k + 1) * LANES]
    d_router[...] = jnp.broadcast_to(tile[...][None], d_router.shape)


def finish_kernel(*refs):
    groups = lax.axis_size("x")
    got = refs[:groups]
    residual, picked, marks, places, block_out, d_queries, d_keys, d_values, block_v, lists_v, sems = refs[groups:]
    _, slots, part = got[0].shape
    tokens, width = residual.shape
    gate, live = marks[:, 0:1], marks[:, 1:2] > 0.0
    own = places[2:3, :slots]
    token = lax.broadcasted_iota(jnp.int32, (tokens, slots), 0).astype(jnp.float32)
    put = (token == own).astype(jnp.float32)
    hit = jnp.sum(put, axis=1, keepdims=True) > 0.0
    put = put.astype(jnp.bfloat16)
    copies = []

    def store(source, target):
        copy = pltpu.make_async_copy(source, target, sems.at[len(copies)])
        copy.start()
        copies.append(copy)

    for distance in range(groups):
        group = lax.rem(lax.axis_index("x") + (groups - distance), groups)
        columns = pl.ds(pl.multiple_of(group * part, part), part)
        for i, out in enumerate((d_queries, d_keys, d_values)):
            lists_v[i, distance] = jnp.where(live, got[distance][1 + i], jnp.zeros((), jnp.bfloat16))
            store(lists_v.at[i, distance], out.at[:, columns])
        att = got[distance][0].astype(jnp.float32)
        mixed = (picked[:, columns].astype(jnp.float32) + gate * att).astype(jnp.bfloat16)
        moved = jnp.dot(put, mixed, preferred_element_type=jnp.float32).astype(jnp.bfloat16)
        block_v[distance] = jnp.where(hit, moved, residual[:, columns])
        store(block_v.at[distance], block_out.at[:, columns])
    for copy in copies:
        copy.wait()


def call(kernel, out_shape, *operands, in_specs, out_specs, scratch_shapes=(), flops):
    outs = out_shape if isinstance(out_shape, tuple) else (out_shape,)
    moved = sum(math.prod(o.shape) * o.dtype.itemsize for o in (*operands, *outs))
    return pl.pallas_call(
        kernel,
        out_shape=out_shape,
        in_specs=in_specs,
        out_specs=out_specs,
        scratch_shapes=scratch_shapes,
        compiler_params=pltpu.CompilerParams(vmem_limit_bytes=24 * MIB),
        cost_estimate=pl.CostEstimate(flops=flops, bytes_accessed=moved, transcendentals=0),
    )(*operands)


def shards(residual, queries, keys, values, grads, router, counts, rows, *, sizes):
    n_y, n_z, n_c, groups = sizes
    tok_dev, width = residual.shape
    slots = queries.shape[0]
    part = width // groups
    bf16, f32 = jnp.bfloat16, jnp.float32
    shape = jax.ShapeDtypeStruct
    packed = shape((groups, 4, slots, part), bf16)
    wide = shape((slots, width), bf16)
    dma = pltpu.SemaphoreType.DMA
    pin = functools.partial(pltpu.with_memory_space_constraint, memory_space=pltpu.HBM)
    router = router.reshape(1, width)
    counts, rows = counts.T, jnp.transpose(rows, (1, 2, 0))
    sent, picked, marks = call(
        functools.partial(prep_kernel, sizes=sizes),
        (pltpu.HBM(packed.shape, bf16), wide, shape((slots, LANES), f32)),
        *(pin(a) for a in (residual, queries, keys, values, grads, router, counts, rows)),
        in_specs=[HBM] * 8,
        out_specs=(HBM, VMEM, VMEM),
        scratch_shapes=[
            pltpu.VMEM((tok_dev, width), bf16),
            pltpu.VMEM((slots, width), bf16),
            pltpu.VMEM((3, slots, width), bf16),
            pltpu.VMEM((1, width), f32),
            pltpu.VMEM(counts.shape, jnp.int32),
            pltpu.VMEM(rows.shape[1:], jnp.int32),
            pltpu.VMEM((groups, slots, part), bf16),
            dma((7 + 5 * groups,)),
        ],
        flops=2 * slots * tok_dev * width,
    )

    def passed(array, distance):
        return lax.ppermute(array, "x", [(i, (i + distance) % groups) for i in range(groups)])

    got = lax.all_to_all(sent, "x", 0, 0)
    n = groups * slots
    places = call(
        functools.partial(places_kernel, sizes=sizes, tok_dev=tok_dev),
        shape((8, n), f32), counts, rows,
        in_specs=[VMEM] * 2, out_specs=VMEM, flops=10 * n * n,
    )
    square = shape((part // LANES, n, n), f32)
    probs, d_probs, dots = call(
        forward_kernel,
        (square, square, shape((groups, 8, n), f32)),
        got, places,
        in_specs=[VMEM] * 2, out_specs=(VMEM,) * 3, flops=4 * n * n * part,
    )
    dots = lax.all_to_all(dots, "x", 0, 0)
    back = call(
        backward_kernel, (pltpu.HBM((4, slots, part), bf16),) * groups, got, probs, d_probs,
        in_specs=[VMEM] * 3, out_specs=(HBM,) * groups,
        scratch_shapes=[pltpu.VMEM((groups, 4, slots, part), bf16), dma((part // LANES // 2 * groups,))],
        flops=8 * n * n * part,
    )
    back = [back[0]] + [passed(back[d], d) for d in range(1, groups)]
    term = call(
        router_kernel, shape((ORDER[0][1](sizes), width // LANES, LANES), f32), dots, picked, marks, pin(back[0]),
        in_specs=[VMEM] * 3 + [HBM], out_specs=VMEM,
        scratch_shapes=[pltpu.VMEM((width // LANES, LANES), f32)], flops=4 * n * width,
    )
    total = jnp.sum(lax.all_to_all(term, ORDER[0][0], 0, 0), axis=0)
    for axes, size in ORDER[1:]:
        copies = jnp.broadcast_to(total[None], (size(sizes), *total.shape))
        total = jnp.sum(lax.all_to_all(copies, axes, 0, 0), axis=0)
    block_out, d_queries, d_keys, d_values = call(
        finish_kernel,
        (shape((tok_dev, width), bf16), wide, wide, wide),
        *back, residual, picked, marks, places,
        in_specs=[VMEM] * (groups + 4),
        out_specs=(ANY,) * 4,
        scratch_shapes=[
            pltpu.VMEM((groups, tok_dev, part), bf16),
            pltpu.VMEM((3, groups, slots, part), bf16),
            dma((4 * groups,)),
        ],
        flops=2 * slots * tok_dev * width,
    )
    return block_out, d_queries, d_keys, d_values, total.reshape(width)


def split_dp(size):
    chips = size // CORES
    z = 2 ** (int(math.log2(chips)) // 2)
    return chips // z, z, CORES


def solution(mesh):
    sizes = (*split_dp(mesh.shape["dp"]), mesh.shape["seq"])
    fine = Mesh(mesh.devices.reshape(sizes), ("y", "z", "c", "x"))
    split = P(("y", "z", "c", "x"), None)
    return jax.shard_map(
        functools.partial(shards, sizes=sizes),
        mesh=fine,
        in_specs=(split,) * 5 + (P(),) * 3,
        out_specs=(split,) * 4 + (P(),),
        check_vma=False,
    )
```
